32 devices in a mesh: section: 4 (over y, x), dom: 8 (over z, core).
Axes of the slice: x: 2, y: 2, z: 4, core: 2. Of those that a mesh axis runs over, the one named last changes fastest.
Arguments:
- features: bfloat16 [2, 2048, 128], P(None, 'dom'), may hold values from -6 to 6
- input_weight: bfloat16 [128, 512], replicated, may hold values from -0.5 to 0.5
- layer_weights: bfloat16 [8, 512, 512], P('section'), may hold values from -0.25 to 0.25
- tiles: bfloat16 [2, 16, 4, 128, 128], P(None, 'dom'), may hold values from -0.4375 to 0.4375
- pub_ids: int32 [2, 16], P(None, 'dom'), may hold values from -1 to 1, as said below
- tile_src: int32 [2, 16, 4], P(None, 'dom'), may hold values from 0 to 5, as said below
Outputs:
- section_outputs: bfloat16 [4, 2, 2048, 512], P('section', None, 'dom')
The draws below stay inside these ranges and needn't reach their ends.
Inputs may be any that keep to these rules, and one draw needn't show every extreme that they name: `pub_ids`: for each node group and partition, its 2 slots hold distinct local block numbers below 2 first and -1 in the unused slots after them; every partition lists at least one block, and in every node group some partition fills all 2 slots. `tile_src`: each entry names a slot of the destination block's partition: a local block below 2, or a listed (not -1) slot of the previous or the next partition; the first partition reads no previous one and the last no next one. In every node group some tile reads the last slot of a next partition.
All inputs are finite; a program needn't handle non-finite values.
Results may differ from the reference program's by a relative error of at most 0.019.
Values may be sent and summed in bfloat16 or wider, within the bound.
No kernel may reach another device: no remote copies, remote signals or barrier semaphores. Data moves between devices by JAX's collectives and lax.ppermute only.
A program may use at most 64 MiB of HBM per device.

```python
import jax
import jax.numpy as jnp
from jax import lax

D = 512
D_IN = 128
BS = 128
NB = 2
K = 4
BMAX = 2
GROUPS = 2
LPS = 2
LAYERS = 8
NBLK = 16
NODES = 2048
N_SECTION = 4
N_DOM = 8


def boundary_plan(key):
    count_key = jax.random.fold_in(key, 101)
    force_key = jax.random.fold_in(key, 102)
    order_key = jax.random.fold_in(key, 103)
    counts = jax.random.randint(count_key, (GROUPS, N_DOM), 1, BMAX + 1)
    forced = jax.random.randint(force_key, (GROUPS,), 1, N_DOM)
    counts = counts.at[jnp.arange(GROUPS), forced].set(BMAX)
    order_keys = jax.random.split(order_key, GROUPS * N_DOM)
    orders = jax.vmap(lambda single: jax.random.permutation(single, NB))(order_keys)
    orders = orders.reshape(GROUPS, N_DOM, NB)[:, :, :BMAX]
    listed = jnp.where(jnp.arange(BMAX)[None, None, :] < counts[:, :, None], orders, -1)
    return (counts.astype(jnp.int32), listed.astype(jnp.int32), forced.astype(jnp.int32))


def draw_pub_ids(key, part):
    counts, listed, forced = boundary_plan(key)
    return listed.reshape(GROUPS, N_DOM * BMAX)


def draw_tile_src(key, part):
    counts, listed, forced = boundary_plan(key)
    block_ids = jnp.arange(N_DOM * NB)
    device = block_ids // NB
    own_block = block_ids % NB
    grid_shape = (GROUPS, N_DOM * NB)
    left_count = counts[:, jnp.clip(device - 1, 0, N_DOM - 1)]
    right_count = counts[:, jnp.clip(device + 1, 0, N_DOM - 1)]
    columns = [jnp.broadcast_to(own_block, grid_shape)]
    columns.append(jax.random.randint(jax.random.fold_in(key, 201), grid_shape, 0, NB))
    left_pick = NB + jax.random.randint(jax.random.fold_in(key, 202), grid_shape, 0, left_count)
    left_other = jax.random.randint(jax.random.fold_in(key, 203), grid_shape, 0, NB)
    columns.append(jnp.where(device[None, :] > 0, left_pick, left_other))
    right_pick = NB + BMAX + jax.random.randint(jax.random.fold_in(key, 204), grid_shape, 0, right_count)
    reach_block = (forced - 1) * NB
    right_pick = jnp.where(block_ids[None, :] == reach_block[:, None], NB + 2 * BMAX - 1, right_pick)
    right_other = jax.random.randint(jax.random.fold_in(key, 205), grid_shape, 0, NB)
    columns.append(jnp.where(device[None, :] < N_DOM - 1, right_pick, right_other))
    for column_index in range(K - 4):
        columns.append(jax.random.randint(jax.random.fold_in(key, 300 + column_index), grid_shape, 0, NB))
    return jnp.stack(columns, -1).astype(jnp.int32)


def shard_levels(key, extent, cuts, smallest, largest):
    def one(axis_at, parts):
        steps = jax.random.uniform(jax.random.fold_in(jax.random.fold_in(key, 6), axis_at), (parts,), jnp.float32, smallest / len(cuts), largest / len(cuts))
        return jnp.repeat(jnp.exp(steps), extent[axis_at] // parts).reshape((-1,) + (1,) * (len(extent) - axis_at - 1))

    loudness = one(*cuts[0])
    for cut in cuts[1:]:
        loudness = loudness * one(*cut)
    return loudness


def centred(stream_key, dims, scale, most, cuts=(), kind=jnp.bfloat16):
    factor_of = shard_levels(stream_key, dims, cuts, -0.22, 0.18) if cuts else 1.0
    result = jax.random.normal(stream_key, dims, jnp.float32) * scale * factor_of
    return jnp.minimum(jnp.maximum(result, -most), most).astype(kind)


def setup_inputs(seed: int = 0) -> dict:
    streams_of = jax.random.split(jax.random.key(seed), 7)
    return {
        "features": centred(streams_of[0], (GROUPS, NODES, D_IN), 1.0, 6.0, ((1, 8),)),
        "input_weight": centred(streams_of[1], (D_IN, D), D_IN ** -0.5, 0.5),
        "layer_weights": centred(streams_of[2], (LAYERS, D, D), D ** -0.5, 0.25, ((0, 4),)),
        "tiles": centred(streams_of[3], (GROUPS, NBLK, K, BS, BS), (1.7 * (K * BS) ** -0.5), 0.4375, ((1, 8),)),
        "pub_ids": draw_pub_ids(jax.random.fold_in(streams_of[6], 71), 0),
        "tile_src": draw_tile_src(jax.random.fold_in(streams_of[6], 71), 0),
    }


residual_share = 0.1
decay_theta = 0.5


def global_sources(source_slots, listed):
    block_total = source_slots.shape[0]
    device = jnp.arange(block_total, dtype=jnp.int32) // NB
    left_dev = jnp.clip(device - 1, 0, N_DOM - 1)
    right_dev = jnp.clip(device + 1, 0, N_DOM - 1)
    middle = jnp.clip(source_slots - NB, 0, BMAX - 1)
    farther = jnp.clip(source_slots - NB - BMAX, 0, BMAX - 1)
    from_left = listed[left_dev[:, None], middle]
    from_right = listed[right_dev[:, None], farther]
    global_ids = jnp.where(source_slots < NB, device[:, None] * NB + source_slots,
                           jnp.where(source_slots < NB + BMAX, left_dev[:, None] * NB + from_left,
                                     right_dev[:, None] * NB + from_right))
    return global_ids.astype(jnp.int32)


def propagate(hidden, initial, group_tiles, global_ids, weight, beta):
    blocks = hidden.reshape(-1, BS, D)

    def per_partition(pair):
        tile_part, id_part = pair
        gathered = jnp.take(blocks, id_part.reshape(-1), axis=0).reshape(NB, K, BS, D)
        return jnp.einsum('bkij,bkjd->bid', tile_part.astype(jnp.float32), gathered.astype(jnp.float32))

    aggregate = lax.map(per_partition, (group_tiles.reshape(N_DOM, NB, K, BS, BS),
                                        global_ids.reshape(N_DOM, NB, K))).reshape(-1, D)
    support = ((1.0 - residual_share) * aggregate + residual_share * initial.astype(jnp.float32)).astype(jnp.bfloat16)
    product = jnp.dot(support, weight, preferred_element_type=jnp.float32)
    mixed = (1.0 - beta) * support.astype(jnp.float32) + beta * product
    return jax.nn.relu(mixed).astype(jnp.bfloat16)


def reference(features, input_weight, layer_weights, tiles, pub_ids, tile_src):
    listed_all = pub_ids.reshape(GROUPS, N_DOM, BMAX)
    results = []
    for group in range(GROUPS):
        initial = jax.nn.relu(jnp.dot(features[group], input_weight, preferred_element_type=jnp.float32)).astype(jnp.bfloat16)
        hidden = initial
        global_ids = global_sources(tile_src[group], listed_all[group])
        per_section = []
        for section_number in range(N_SECTION):
            for inner in range(LPS):
                layer = section_number * LPS + inner
                beta = jnp.log(decay_theta / jnp.float32(layer + 1) + 1.0)
                hidden = propagate(hidden, initial, tiles[group], global_ids, layer_weights[layer], beta)
            per_section.append(hidden)
        results.append(jnp.stack(per_section))
    return jnp.stack(results, axis=1)
```

```python
import functools
import math

import jax
import jax.numpy as jnp
from jax import lax
from jax.experimental import pallas as pl
from jax.experimental.pallas import tpu as pltpu
from jax.sharding import PartitionSpec as P

residual_share = 0.1
decay_theta = 0.5
vmem_bytes = 44 * 2**20
meta_rows = 32


def swapped(block, axis, mask):
    return lax.ppermute(block, axis, [(i, i ^ mask) for i in range(lax.axis_size(axis))])


def shifted(block, axis, distance):
    devices = range(lax.axis_size(axis))
    return lax.ppermute(block, axis, [(i + distance, i) for i in devices if i + distance in devices])


def one_way(block, axis, pairs):
    return lax.ppermute(block, axis, pairs)


def cone_kernel(dims, *refs):
    (parts, in_order, layers, per_section, blocks, tile_count, listed_count, tile_rows, rows, slots, shares) = dims
    place_ref, entry_ref = refs[:2]
    pieces = refs[2 : 2 + parts]
    inputs = refs[2 + parts : 2 + parts + len(shares)]
    placed_ref, sent_ref = refs[2 + parts + len(shares) : 4 + parts + len(shares)]
    layer_weight, band, initial, even, odd, notes, plan, sems, plan_sem = refs[4 + parts + len(shares) :]
    own, section, core, group = [place_ref[i] for i in range(4)]
    states = (even, odd)
    tile_area = blocks * tile_count * tile_rows

    def copy(index):
        mask, flip = shares[index]
        target = layer_weight.at[pl.ds((section ^ mask) * per_section, per_section)]
        if flip is not None:
            size = inputs[index].shape[1]
            target = target.at[:, pl.ds(pl.multiple_of((core ^ flip) * size, size), size)]
        return pltpu.make_async_copy(inputs[index], target, sems.at[index])

    for index in range(len(inputs)):
        copy(index).start()
    for slot in range(parts):
        line = pieces[slot][tile_area + rows :].astype(jnp.float32)
        notes[slot : slot + 1] = line[0:1].astype(jnp.int32)
    to_scalars = pltpu.make_async_copy(notes, plan, plan_sem)
    to_scalars.start()
    empty = jnp.zeros((rows, even.shape[1]), jnp.bfloat16)
    for state in states:
        state[0:rows] = empty
        state[(parts + 1) * rows : (parts + 2) * rows] = empty

    def slot_of(position):
        return position if in_order else position ^ own

    for slot in range(parts):
        position = slot_of(slots[slot])
        value = jnp.dot(pieces[slot][tile_area : tile_area + rows], entry_ref[...], preferred_element_type=jnp.float32)
        value = jnp.maximum(value, 0.0).astype(jnp.bfloat16)
        initial[position] = value
        even[pl.ds(pl.multiple_of((position + 1) * rows, rows), rows)] = value
    to_scalars.wait()

    order = {slot: index for index, slot in enumerate(slots)}

    def note(slot, index):
        if in_order:
            return plan[slot, index]
        found = plan[0, index]
        for which in range(1, parts):
            found = jnp.where(slot == slots[which], plan[which, index], found)
        return found

    for index, slot in enumerate(slots):
        position = slot_of(slot)
        before = slot_of(jnp.maximum(position - 1, 0))
        after = slot_of(jnp.minimum(position + 1, parts - 1))
        previous = [note(before, i) for i in range(listed_count)]
        following = [note(after, i) for i in range(listed_count)]
        band[position] = jnp.zeros(band.shape[1:], jnp.bfloat16)
        for block in range(blocks):
            for k in range(tile_count):
                source = plan[index, listed_count + block * tile_count + k]
                far = source - blocks
                column = blocks + source
                for i in range(listed_count):
                    column = jnp.where(far == i, previous[i], column)
                    column = jnp.where(far == listed_count + i, 2 * blocks + following[i], column)
                column = jnp.clip(column, 0, 3 * blocks - 1)
                start = pl.multiple_of(column * tile_rows, tile_rows)
                first = (block * tile_count + k) * tile_rows
                place = (position, slice(block * tile_rows, (block + 1) * tile_rows), pl.ds(start, tile_rows))
                band[place] += pieces[index][first : first + tile_rows]

    for index in range(len(inputs)):
        copy(index).wait()

    for layer in range(layers):
        beta = math.log(decay_theta / (layer + 1) + 1.0)
        reach = layers - 1 - layer
        count = min(parts, 2 * reach + 1)
        base = 0 if count == parts else jnp.clip(own - reach, 0, parts - count)
        before_ref, after_ref = states[layer % 2], states[(layer + 1) % 2]

        def advance(position, before_ref=before_ref, after_ref=after_ref, beta=beta, layer=layer):
            window = before_ref[pl.ds(pl.multiple_of(position * rows, rows), 3 * rows)]
            aggregate = jnp.dot(band[position], window, preferred_element_type=jnp.float32)
            support = (
                (1.0 - residual_share) * aggregate + residual_share * initial[position].astype(jnp.float32)
            ).astype(jnp.bfloat16)
            product = jnp.dot(support, layer_weight[layer], preferred_element_type=jnp.float32)
            mixed = (1.0 - beta) * support.astype(jnp.float32) + beta * product
            target = pl.ds(pl.multiple_of((position + 1) * rows, rows), rows)
            after_ref[target] = jnp.maximum(mixed, 0.0).astype(jnp.bfloat16)

        if in_order:
            pl.loop(base, base + count)(advance)
        else:
            for step in range(count):
                advance(base + step)
        if (layer + 1) % per_section == 0:
            leaving = layer // per_section
            mine = pl.ds(pl.multiple_of((own + 1) * rows, rows), rows)

            @pl.when(section == leaving)
            def _():
                placed_ref[0, group] = after_ref[mine]

            @pl.when(section ^ 1 == leaving)
            def _():
                sent_ref[...] = after_ref[mine]


def shards(features, input_weight, layer_weights, tiles, pub_ids, tile_src):
    groups, rows, _ = features.shape
    _, blocks, tile_count, tile_rows, _ = tiles.shape
    listed_count = pub_ids.shape[1]
    per_section, width, _ = layer_weights.shape
    section, sections = lax.axis_index("section"), lax.axis_size("section")
    me, doms = lax.axis_index("dom"), lax.axis_size("dom")
    layers = per_section * sections
    core, group = me % 2, section % groups

    half = width // 2
    my_share = lax.dynamic_slice_in_dim(layer_weights, core * half, half, 1)
    own_tiles = lax.dynamic_index_in_dim(tiles, group, 0, keepdims=False).reshape(-1, tile_rows)
    own_features = lax.dynamic_index_in_dim(features, group, 0, keepdims=False)
    own_ids = lax.dynamic_index_in_dim(pub_ids, group, 0, keepdims=False)
    own_sources = lax.dynamic_index_in_dim(tile_src, group, 0, keepdims=False).reshape(-1)
    notes = jnp.concatenate([own_ids, own_sources])
    notes = jnp.pad(notes.astype(jnp.bfloat16)[None], ((0, meta_rows - 1), (0, tile_rows - notes.shape[0])))
    payload = jnp.concatenate([own_tiles, own_features, notes], 0)
    payload, my_share = lax.optimization_barrier((payload, my_share))

    in_order = doms > layers or doms & (doms - 1) != 0
    lower = range(sections // 2)
    if in_order:
        parts, own = 2 * layers + 1, jnp.int32(layers)
        slots = tuple(range(parts))
        pieces = [payload if d == 0 else shifted(payload, "dom", d) for d in range(-layers, layers + 1)]
        first = pieces[0]
    else:
        parts, own = doms, me
        direct = {mask: swapped(payload, "dom", mask) for mask in reversed(range(2, parts, 2))}
        first = direct[2]
        slots, pieces = [0, 1], [payload, swapped(payload, "dom", 1)]
        for mask in range(2, parts, 2):
            slots += [mask, mask + 1]
            pieces += [direct[mask], swapped(direct[mask], "dom", 1)]
        slots = tuple(slots)
    received = []
    for mask in range(sections - 1, 1, -1):
        pairs = [(i, i ^ mask) for i in lower if i ^ mask not in lower]
        received.append((mask, one_way(my_share, "section", pairs)))
    later_share, _ = lax.optimization_barrier((my_share, first))
    received.append((1, swapped(later_share, "section", 1)))
    inputs, shares = [layer_weights], [(0, None)]
    for mask, share in received:
        inputs += [share, swapped(share, "dom", 1)]
        shares += [(mask, 0), (mask, 1)]
    place = jnp.stack([own, section, core, group]).astype(jnp.int32)

    dims = (
        parts, in_order, layers, per_section, blocks, tile_count, listed_count, tile_rows, rows, slots, tuple(shares),
    )
    smem = pl.BlockSpec(memory_space=pltpu.SMEM)
    vmem = pl.BlockSpec(memory_space=pltpu.VMEM)
    anywhere = pl.BlockSpec(memory_space=pl.ANY)
    placed, sent = pl.pallas_call(
        functools.partial(cone_kernel, dims),
        out_shape=(
            jax.ShapeDtypeStruct((1, groups, rows, width), jnp.bfloat16),
            jax.ShapeDtypeStruct((rows, width), jnp.bfloat16),
        ),
        in_specs=[smem, vmem] + [vmem] * parts + [anywhere] * len(inputs),
        out_specs=(vmem, vmem),
        scratch_shapes=[
            pltpu.VMEM((layers, width, width), jnp.bfloat16),
            pltpu.VMEM((parts, rows, 3 * rows), jnp.bfloat16),
            pltpu.VMEM((parts, rows, width), jnp.bfloat16),
            pltpu.VMEM(((parts + 2) * rows, width), jnp.bfloat16),
            pltpu.VMEM(((parts + 2) * rows, width), jnp.bfloat16),
            pltpu.VMEM((parts, tile_rows), jnp.int32),
            pltpu.SMEM((parts, tile_rows), jnp.int32),
            pltpu.SemaphoreType.DMA((len(inputs),)),
            pltpu.SemaphoreType.DMA,
        ],
        compiler_params=pltpu.CompilerParams(vmem_limit_bytes=vmem_bytes),
    )(place, input_weight, *pieces, *inputs)
    other = swapped(sent, "section", 1)
    return lax.dynamic_update_slice(placed, other[None, None], (0, 1 - group, 0, 0))


def solution(mesh):
    in_specs = (
        P(None, "dom", None),
        P(),
        P("section", None, None),
        P(None, "dom", None, None, None),
        P(None, "dom"),
        P(None, "dom", None),
    )
    out_specs = P("section", None, "dom", None)
    return jax.shard_map(shards, mesh=mesh, in_specs=in_specs, out_specs=out_specs, check_vma=False)
```

```python
import functools
import math

import jax
import jax.numpy as jnp
from jax import lax
from jax.experimental import pallas as pl
from jax.experimental.pallas import tpu as pltpu
from jax.sharding import PartitionSpec as P

residual_share = 0.1
decay_theta = 0.5
vmem_bytes = 44 * 2**20
meta_rows = 16


def swapped(block, axis, mask):
    return lax.ppermute(block, axis, [(i, i ^ mask) for i in range(lax.axis_size(axis))])


def shifted(block, axis, distance):
    devices = range(lax.axis_size(axis))
    return lax.ppermute(block, axis, [(i + distance, i) for i in devices if i + distance in devices])


def one_way(block, axis, pairs):
    return lax.ppermute(block, axis, pairs)


def cone_kernel(dims, *refs):
    (parts, in_order, layers, per_section, blocks, tile_count, listed_count, tile_rows, rows, slots, shares, lower) = dims
    place_ref, entry_ref = refs[:2]
    pieces = refs[2 : 2 + parts]
    inputs = refs[2 + parts : 2 + parts + len(shares)]
    placed_ref, sent_ref = refs[2 + parts + len(shares) : 4 + parts + len(shares)]
    layer_weight, band, initial, even, odd, first_support, second_support, notes, plan, sems, plan_sem = refs[4 + parts + len(shares) :]
    own, section, core, group = [place_ref[i] for i in range(4)]
    states = (even, odd)
    tile_area = blocks * tile_count * tile_rows

    def copy(index):
        kind, flip = shares[index]
        if kind == "up":
            place = ((section ^ core) & 1) ^ flip
            place = jnp.where(section < lower, lower + place, place)
            target = layer_weight.at[pl.ds(place * per_section, per_section)]
        else:
            owner = section ^ 1 if kind == "pair" else section
            target = layer_weight.at[pl.ds(owner * per_section, per_section)]
            if flip is not None:
                size = inputs[index].shape[1]
                target = target.at[:, pl.ds(pl.multiple_of((core ^ flip) * size, size), size)]
        return pltpu.make_async_copy(inputs[index], target, sems.at[index])

    for index in range(len(inputs)):
        copy(index).start()
    for slot in range(parts):
        line = pieces[slot][tile_area + rows :].astype(jnp.float32)
        notes[slot : slot + 1] = line[0:1].astype(jnp.int32)
    to_scalars = pltpu.make_async_copy(notes, plan, plan_sem)
    to_scalars.start()
    empty = jnp.zeros((rows, even.shape[1]), jnp.bfloat16)
    for state in states:
        state[0:rows] = empty
        state[(parts + 1) * rows : (parts + 2) * rows] = empty

    def slot_of(position):
        return position if in_order else position ^ own

    for slot in range(parts):
        position = slot_of(slots[slot])
        value = jnp.dot(pieces[slot][tile_area : tile_area + rows], entry_ref[...], preferred_element_type=jnp.float32)
        value = jnp.maximum(value, 0.0).astype(jnp.bfloat16)
        initial[position] = value
        even[pl.ds(pl.multiple_of((position + 1) * rows, rows), rows)] = value
    to_scalars.wait()

    order = {slot: index for index, slot in enumerate(slots)}

    def note(slot, index):
        if in_order:
            return plan[slot, index]
        found = plan[0, index]
        for which in range(1, parts):
            found = jnp.where(slot == slots[which], plan[which, index], found)
        return found

    for index, slot in enumerate(slots):
        position = slot_of(slot)
        before = slot_of(jnp.maximum(position - 1, 0))
        after = slot_of(jnp.minimum(position + 1, parts - 1))
        previous = [note(before, i) for i in range(listed_count)]
        following = [note(after, i) for i in range(listed_count)]
        band[position] = jnp.zeros(band.shape[1:], jnp.bfloat16)
        for block in range(blocks):
            for k in range(tile_count):
                source = plan[index, listed_count + block * tile_count + k]
                far = source - blocks
                column = blocks + source
                for i in range(listed_count):
                    column = jnp.where(far == i, previous[i], column)
                    column = jnp.where(far == listed_count + i, 2 * blocks + following[i], column)
                column = jnp.clip(column, 0, 3 * blocks - 1)
                start = pl.multiple_of(column * tile_rows, tile_rows)
                first = (block * tile_count + k) * tile_rows
                place = (position, slice(block * tile_rows, (block + 1) * tile_rows), pl.ds(start, tile_rows))
                band[place] += pieces[index][first : first + tile_rows]

    raised = [index for index, share in enumerate(shares) if share[0] == "up"]
    homes = [index for index, share in enumerate(shares) if share[0] != "up"]

    @pl.when(section >= lower)
    def _():
        for index in raised:
            copy(index).wait()

    @pl.when(section < lower)
    def _():
        for index in homes:
            copy(index).wait()

    depth = jnp.where(section < lower, lower * per_section, layers)
    for layer in range(layers):
        beta = math.log(decay_theta / (layer + 1) + 1.0)
        reach = depth - 1 - layer
        lowest = jnp.maximum(own - reach, 0)
        highest = jnp.minimum(own + reach + 1, parts)
        count = jnp.where(reach >= 0, highest - lowest, 0)
        before_ref, after_ref = states[layer % 2], states[(layer + 1) % 2]
        if layer == lower * per_section:

            @pl.when(section >= lower)
            def _():
                for index in homes:
                    copy(index).wait()

            @pl.when(section < lower)
            def _():
                for index in raised:
                    copy(index).wait()

        def support_of(position, before_ref=before_ref):
            window = before_ref[pl.ds(pl.multiple_of(position * rows, rows), 3 * rows)]
            aggregate = jnp.dot(band[position], window, preferred_element_type=jnp.float32)
            return (
                (1.0 - residual_share) * aggregate + residual_share * initial[position].astype(jnp.float32)
            ).astype(jnp.bfloat16)

        def finish(position, support, after_ref=after_ref, beta=beta, layer=layer):
            product = jnp.dot(support, layer_weight[layer], preferred_element_type=jnp.float32)
            mixed = (1.0 - beta) * support.astype(jnp.float32) + beta * product
            target = pl.ds(pl.multiple_of((position + 1) * rows, rows), rows)
            after_ref[target] = jnp.maximum(mixed, 0.0).astype(jnp.bfloat16)

        partial = count > 0
        if not in_order and 2 * (layers - 1 - layer) + 1 >= parts:
            partial = partial & (count < parts)

            @pl.when(count == parts)
            def _(support_of=support_of, finish=finish):
                for position in range(parts):
                    finish(position, support_of(position))

        @pl.when(partial)
        def _(support_of=support_of, finish=finish, lowest=lowest, highest=highest, count=count):
            first_support[...] = support_of(lowest)

            @pl.loop(0, count // 2)
            def _(pair):
                position = lowest + 2 * pair
                second_support[...] = support_of(position + 1)
                finish(position, first_support[...])
                first_support[...] = support_of(jnp.minimum(position + 2, highest - 1))
                finish(position + 1, second_support[...])

            @pl.when(count % 2 == 1)
            def _():
                finish(highest - 1, first_support[...])

        if (layer + 1) % per_section == 0:
            leaving = layer // per_section
            mine = pl.ds(pl.multiple_of((own + 1) * rows, rows), rows)

            @pl.when(section == leaving)
            def _():
                placed_ref[0, group] = after_ref[mine]

            @pl.when(section ^ 1 == leaving)
            def _():
                sent_ref[...] = after_ref[mine]


def shards(features, input_weight, layer_weights, tiles, pub_ids, tile_src):
    groups, rows, _ = features.shape
    _, blocks, tile_count, tile_rows, _ = tiles.shape
    listed_count = pub_ids.shape[1]
    per_section, width, _ = layer_weights.shape
    section, sections = lax.axis_index("section"), lax.axis_size("section")
    me, doms = lax.axis_index("dom"), lax.axis_size("dom")
    layers = per_section * sections
    core, group = me % 2, section % groups

    own_tiles = lax.dynamic_index_in_dim(tiles, group, 0, keepdims=False).reshape(-1, tile_rows)
    own_features = lax.dynamic_index_in_dim(features, group, 0, keepdims=False)
    own_ids = lax.dynamic_index_in_dim(pub_ids, group, 0, keepdims=False)
    own_sources = lax.dynamic_index_in_dim(tile_src, group, 0, keepdims=False).reshape(-1)
    notes = jnp.concatenate([own_ids, own_sources])
    notes = jnp.pad(notes.astype(jnp.bfloat16)[None], ((0, meta_rows - 1), (0, tile_rows - notes.shape[0])))
    payload = jnp.concatenate([own_tiles, own_features, notes], 0)
    payload, layer_weights = lax.optimization_barrier((payload, layer_weights))

    in_order = doms > layers or doms & (doms - 1) != 0
    lower = sections // 2
    senders = [(t, d) for t in range(lower) for d in range(doms)]
    route = [(t * doms + d, (lower + (t ^ d % 2)) * doms + d) for t, d in senders]
    half = width // 2
    my_share = lax.dynamic_slice_in_dim(layer_weights, core * half, half, 1)
    masks = () if in_order else range(2, doms, 2)
    far = [swapped(payload, "dom", mask) for mask in masks]
    up = one_way(layer_weights, ("section", "dom"), route)
    pair = swapped(my_share, "section", 1)
    mate = swapped(payload, "dom", 1)
    far, up, pair, mate = lax.optimization_barrier((far, up, pair, mate))
    if in_order:
        parts, own = 2 * layers + 1, jnp.int32(layers)
        slots = tuple(range(parts))
        pieces = [payload if d == 0 else shifted(payload, "dom", d) for d in range(-layers, layers + 1)]
    else:
        parts, own = doms, me
        slots, pieces = [0, 1], [payload, mate]
        for mask, piece in zip(masks, far):
            slots += [mask, mask + 1]
            pieces += [piece, swapped(piece, "dom", 1)]
        slots = tuple(slots)
    inputs = [layer_weights, up, swapped(up, "dom", 1), pair, swapped(pair, "dom", 1)]
    shares = [("own", None), ("up", 0), ("up", 1), ("pair", 0), ("pair", 1)]
    place = jnp.stack([own, section, core, group]).astype(jnp.int32)

    dims = (
        parts, in_order, layers, per_section, blocks, tile_count, listed_count, tile_rows, rows, slots, tuple(shares), lower,
    )
    smem = pl.BlockSpec(memory_space=pltpu.SMEM)
    vmem = pl.BlockSpec(memory_space=pltpu.VMEM)
    anywhere = pl.BlockSpec(memory_space=pl.ANY)
    placed, sent = pl.pallas_call(
        functools.partial(cone_kernel, dims),
        out_shape=(
            jax.ShapeDtypeStruct((1, groups, rows, width), jnp.bfloat16),
            jax.ShapeDtypeStruct((rows, width), jnp.bfloat16),
        ),
        in_specs=[smem, vmem] + [vmem] * parts + [anywhere] * len(inputs),
        out_specs=(vmem, vmem),
        scratch_shapes=[
            pltpu.VMEM((layers, width, width), jnp.bfloat16),
            pltpu.VMEM((parts, rows, 3 * rows), jnp.bfloat16),
            pltpu.VMEM((parts, rows, width), jnp.bfloat16),
            pltpu.VMEM(((parts + 2) * rows, width), jnp.bfloat16),
            pltpu.VMEM(((parts + 2) * rows, width), jnp.bfloat16),
            pltpu.VMEM((rows, width), jnp.bfloat16),
            pltpu.VMEM((rows, width), jnp.bfloat16),
            pltpu.VMEM((parts, tile_rows), jnp.int32),
            pltpu.SMEM((parts, tile_rows), jnp.int32),
            pltpu.SemaphoreType.DMA((len(inputs),)),
            pltpu.SemaphoreType.DMA,
        ],
        compiler_params=pltpu.CompilerParams(vmem_limit_bytes=vmem_bytes),
    )(place, input_weight, *pieces, *inputs)
    other = swapped(sent, "section", 1)
    return lax.dynamic_update_slice(placed, other[None, None], (0, 1 - group, 0, 0))


def solution(mesh):
    in_specs = (
        P(None, "dom", None),
        P(),
        P("section", None, None),
        P(None, "dom", None, None, None),
        P(None, "dom"),
        P(None, "dom", None),
    )
    out_specs = P("section", None, "dom", None)
    return jax.shard_map(shards, mesh=mesh, in_specs=in_specs, out_specs=out_specs, check_vma=False)
```

```python
import functools
import math

import jax
import jax.numpy as jnp
from jax import lax
from jax.experimental import pallas as pl
from jax.experimental.pallas import tpu as pltpu
from jax.sharding import PartitionSpec as P

residual_share = 0.1
decay_theta = 0.5
vmem_bytes = 44 * 2**20
meta_rows = 16


def swapped(block, axis, mask):
    return lax.ppermute(block, axis, [(i, i ^ mask) for i in range(lax.axis_size(axis))])


def shifted(block, axis, distance):
    devices = range(lax.axis_size(axis))
    return lax.ppermute(block, axis, [(i + distance, i) for i in devices if i + distance in devices])


def one_way(block, axis, pairs):
    return lax.ppermute(block, axis, pairs)


def cone_kernel(dims, *refs):
    (parts, in_order, layers, per_section, blocks, tile_count, listed_count, tile_rows, rows, slots, shares, lower) = dims
    place_ref, entry_ref = refs[:2]
    pieces = refs[2 : 2 + parts]
    inputs = refs[2 + parts : 2 + parts + len(shares)]
    placed_ref, sent_ref = refs[2 + parts + len(shares) : 4 + parts + len(shares)]
    layer_weight, band, initial, even, odd, first_support, second_support, notes, plan, sems, plan_sem = refs[4 + parts + len(shares) :]
    own, section, core, group = [place_ref[i] for i in range(4)]
    states = (even, odd)
    tile_area = blocks * tile_count * tile_rows

    def copy(index):
        kind, flip = shares[index]
        if kind == "up":
            place = ((section ^ core) & 1) ^ flip
            place = jnp.where(section < lower, lower + place, place)
            target = layer_weight.at[pl.ds(place * per_section, per_section)]
        else:
            owner = section ^ 1 if kind == "pair" else section
            target = layer_weight.at[pl.ds(owner * per_section, per_section)]
            if flip is not None:
                size = inputs[index].shape[1]
                target = target.at[:, pl.ds(pl.multiple_of((core ^ flip) * size, size), size)]
        return pltpu.make_async_copy(inputs[index], target, sems.at[index])

    for index in range(len(inputs)):
        copy(index).start()
    for slot in range(parts):
        line = pieces[slot][tile_area + rows :].astype(jnp.float32)
        notes[slot : slot + 1] = line[0:1].astype(jnp.int32)
    to_scalars = pltpu.make_async_copy(notes, plan, plan_sem)
    to_scalars.start()
    empty = jnp.zeros((rows, even.shape[1]), jnp.bfloat16)
    for state in states:
        state[0:rows] = empty
        state[(parts + 1) * rows : (parts + 2) * rows] = empty

    def slot_of(position):
        return position if in_order else position ^ own

    for slot in range(parts):
        position = slot_of(slots[slot])
        value = jnp.dot(pieces[slot][tile_area : tile_area + rows], entry_ref[...], preferred_element_type=jnp.float32)
        value = jnp.maximum(value, 0.0).astype(jnp.bfloat16)
        initial[position] = value
        even[pl.ds(pl.multiple_of((position + 1) * rows, rows), rows)] = value
    to_scalars.wait()

    def note(slot, index):
        if in_order:
            return plan[slot, index]
        found = plan[0, index]
        for which in range(1, parts):
            found = jnp.where(slot == slots[which], plan[which, index], found)
        return found

    for index, slot in enumerate(slots):
        position = slot_of(slot)
        before = slot_of(jnp.maximum(position - 1, 0))
        after = slot_of(jnp.minimum(position + 1, parts - 1))
        previous = [note(before, i) for i in range(listed_count)]
        following = [note(after, i) for i in range(listed_count)]
        band[position] = jnp.zeros(band.shape[1:], jnp.bfloat16)
        for block in range(blocks):
            for k in range(tile_count):
                source = plan[index, listed_count + block * tile_count + k]
                far = source - blocks
                column = blocks + source
                for i in range(listed_count):
                    column = jnp.where(far == i, previous[i], column)
                    column = jnp.where(far == listed_count + i, 2 * blocks + following[i], column)
                column = jnp.clip(column, 0, 3 * blocks - 1)
                start = pl.multiple_of(column * tile_rows, tile_rows)
                first = (block * tile_count + k) * tile_rows
                place = (position, slice(block * tile_rows, (block + 1) * tile_rows), pl.ds(start, tile_rows))
                band[place] += pieces[index][first : first + tile_rows]

    raised = [index for index, share in enumerate(shares) if share[0] == "up"]
    homes = [index for index, share in enumerate(shares) if share[0] != "up"]

    @pl.when(section >= lower)
    def _():
        for index in raised:
            copy(index).wait()

    @pl.when(section < lower)
    def _():
        for index in homes:
            copy(index).wait()

    depth = jnp.where(section < lower, lower * per_section, layers)
    for layer in range(layers):
        beta = math.log(decay_theta / (layer + 1) + 1.0)
        reach = depth - 1 - layer
        lowest = jnp.maximum(own - reach, 0)
        highest = jnp.minimum(own + reach + 1, parts)
        count = jnp.where(reach >= 0, highest - lowest, 0)
        before_ref, after_ref = states[layer % 2], states[(layer + 1) % 2]
        if layer == lower * per_section:

            @pl.when(section >= lower)
            def _():
                for index in homes:
                    copy(index).wait()

            @pl.when(section < lower)
            def _():
                for index in raised:
                    copy(index).wait()

        def support_of(position, before_ref=before_ref):
            window = before_ref[pl.ds(pl.multiple_of(position * rows, rows), 3 * rows)]
            aggregate = jnp.dot(band[position], window, preferred_element_type=jnp.float32)
            return (
                (1.0 - residual_share) * aggregate + residual_share * initial[position].astype(jnp.float32)
            ).astype(jnp.bfloat16)

        def finish(position, support, after_ref=after_ref, beta=beta, layer=layer):
            product = jnp.dot(support, layer_weight[layer], preferred_element_type=jnp.float32)
            mixed = (1.0 - beta) * support.astype(jnp.float32) + beta * product
            target = pl.ds(pl.multiple_of((position + 1) * rows, rows), rows)
            after_ref[target] = jnp.maximum(mixed, 0.0).astype(jnp.bfloat16)

        partial = count > 0
        if not in_order and 2 * (layers - 1 - layer) + 1 >= parts:
            partial = partial & (count < parts)

            @pl.when(count == parts)
            def _(support_of=support_of, finish=finish):
                for position in range(parts):
                    finish(position, support_of(position))

        @pl.when(partial)
        def _(support_of=support_of, finish=finish, lowest=lowest, highest=highest, count=count):
            first_support[...] = support_of(lowest)

            @pl.loop(0, count // 2)
            def _(pair):
                position = lowest + 2 * pair
                second_support[...] = support_of(position + 1)
                finish(position, first_support[...])
                first_support[...] = support_of(jnp.minimum(position + 2, highest - 1))
                finish(position + 1, second_support[...])

            @pl.when(count % 2 == 1)
            def _():
                finish(highest - 1, first_support[...])

        if (layer + 1) % per_section == 0:
            leaving = layer // per_section
            mine = pl.ds(pl.multiple_of((own + 1) * rows, rows), rows)

            @pl.when(section == leaving)
            def _():
                placed_ref[0, group] = after_ref[mine]

            @pl.when(section ^ 1 == leaving)
            def _():
                sent_ref[...] = after_ref[mine]


def shards(features, input_weight, layer_weights, tiles, pub_ids, tile_src):
    groups, rows, _ = features.shape
    _, blocks, tile_count, tile_rows, _ = tiles.shape
    listed_count = pub_ids.shape[1]
    per_section, width, _ = layer_weights.shape
    section, sections = lax.axis_index("section"), lax.axis_size("section")
    me, doms = lax.axis_index("dom"), lax.axis_size("dom")
    layers = per_section * sections
    core, group = me % 2, section % groups

    own_tiles = lax.dynamic_index_in_dim(tiles, group, 0, keepdims=False).reshape(-1, tile_rows)
    own_features = lax.dynamic_index_in_dim(features, group, 0, keepdims=False)
    own_ids = lax.dynamic_index_in_dim(pub_ids, group, 0, keepdims=False)
    own_sources = lax.dynamic_index_in_dim(tile_src, group, 0, keepdims=False).reshape(-1)
    notes = jnp.concatenate([own_ids, own_sources])
    notes = jnp.pad(notes.astype(jnp.bfloat16)[None], ((0, meta_rows - 1), (0, tile_rows - notes.shape[0])))
    payload = jnp.concatenate([own_tiles, own_features, notes], 0)
    payload, layer_weights = lax.optimization_barrier((payload, layer_weights))

    in_order = doms > layers or doms & (doms - 1) != 0
    lower = sections // 2
    senders = [(t, d) for t in range(lower) for d in range(doms)]
    route = [(t * doms + d, (lower + (t ^ d % 2)) * doms + d) for t, d in senders]
    half = width // 2
    my_share = lax.dynamic_slice_in_dim(layer_weights, core * half, half, 1)
    masks = () if in_order else range(2, doms, 2)
    far = [swapped(payload, "dom", mask) for mask in masks]
    up = one_way(layer_weights, ("section", "dom"), route)
    pair = swapped(my_share, "section", 1)
    far = lax.optimization_barrier(far)
    if in_order:
        parts, own = 2 * layers + 1, jnp.int32(layers)
        slots = tuple(range(parts))
        pieces = [payload if d == 0 else shifted(payload, "dom", d) for d in range(-layers, layers + 1)]
    else:
        parts, own = doms, me
        slots, pieces = [0, 1], [payload, swapped(payload, "dom", 1)]
        for mask, piece in zip(masks, far):
            slots += [mask, mask + 1]
            pieces += [piece, swapped(piece, "dom", 1)]
        pair, _ = lax.optimization_barrier((pair, pieces[3::2]))
        slots = tuple(slots)
    inputs = [layer_weights, up, swapped(up, "dom", 1), pair, swapped(pair, "dom", 1)]
    shares = [("own", None), ("up", 0), ("up", 1), ("pair", 0), ("pair", 1)]
    place = jnp.stack([own, section, core, group]).astype(jnp.int32)

    dims = (
        parts, in_order, layers, per_section, blocks, tile_count, listed_count, tile_rows, rows, slots, tuple(shares), lower,
    )
    smem = pl.BlockSpec(memory_space=pltpu.SMEM)
    vmem = pl.BlockSpec(memory_space=pltpu.VMEM)
    anywhere = pl.BlockSpec(memory_space=pl.ANY)
    placed, sent = pl.pallas_call(
        functools.partial(cone_kernel, dims),
        out_shape=(
            jax.ShapeDtypeStruct((1, groups, rows, width), jnp.bfloat16),
            jax.ShapeDtypeStruct((rows, width), jnp.bfloat16),
        ),
        in_specs=[smem, vmem] + [vmem] * parts + [anywhere] * len(inputs),
        out_specs=(vmem, vmem),
        scratch_shapes=[
            pltpu.VMEM((layers, width, width), jnp.bfloat16),
            pltpu.VMEM((parts, rows, 3 * rows), jnp.bfloat16),
            pltpu.VMEM((parts, rows, width), jnp.bfloat16),
            pltpu.VMEM(((parts + 2) * rows, width), jnp.bfloat16),
            pltpu.VMEM(((parts + 2) * rows, width), jnp.bfloat16),
            pltpu.VMEM((rows, width), jnp.bfloat16),
            pltpu.VMEM((rows, width), jnp.bfloat16),
            pltpu.VMEM((parts, tile_rows), jnp.int32),
            pltpu.SMEM((parts, tile_rows), jnp.int32),
            pltpu.SemaphoreType.DMA((len(inputs),)),
            pltpu.SemaphoreType.DMA,
        ],
        compiler_params=pltpu.CompilerParams(vmem_limit_bytes=vmem_bytes),
    )(place, input_weight, *pieces, *inputs)
    other = swapped(sent, "section", 1)
    return lax.dynamic_update_slice(placed, other[None, None], (0, 1 - group, 0, 0))


def solution(mesh):
    in_specs = (
        P(None, "dom", None),
        P(),
        P("section", None, None),
        P(None, "dom", None, None, None),
        P(None, "dom"),
        P(None, "dom", None),
    )
    out_specs = P("section", None, "dom", None)
    return jax.shard_map(shards, mesh=mesh, in_specs=in_specs, out_specs=out_specs, check_vma=False)
```

```python
import functools
import math

import jax
import jax.numpy as jnp
from jax import lax
from jax.experimental import pallas as pl
from jax.experimental.pallas import tpu as pltpu
from jax.sharding import PartitionSpec as P

residual_share = 0.1
decay_theta = 0.5
vmem_bytes = 44 * 2**20
meta_rows = 16


def swapped(block, axis, mask):
    return lax.ppermute(block, axis, [(i, i ^ mask) for i in range(lax.axis_size(axis))])


def shifted(block, axis, distance):
    devices = range(lax.axis_size(axis))
    return lax.ppermute(block, axis, [(i + distance, i) for i in devices if i + distance in devices])


def one_way(block, axis, pairs):
    return lax.ppermute(block, axis, pairs)


def cone_kernel(dims, *refs):
    (parts, in_order, layers, per_section, blocks, tile_count, listed_count, tile_rows, rows, slots, shares, lower) = dims
    place_ref, entry_ref = refs[:2]
    pieces = refs[2 : 2 + parts]
    inputs = refs[2 + parts : 2 + parts + len(shares)]
    placed_ref, sent_ref = refs[2 + parts + len(shares) : 4 + parts + len(shares)]
    layer_weight, band, initial, even, odd, first_support, second_support, notes, plan, sems, plan_sem = refs[4 + parts + len(shares) :]
    own, section, core, group = [place_ref[i] for i in range(4)]
    states = (even, odd)
    tile_area = blocks * tile_count * tile_rows

    def copy(index):
        kind, flip = shares[index]
        if kind == "up":
            place = ((section ^ core) & 1) ^ flip
            place = jnp.where(section < lower, lower + place, place)
            target = layer_weight.at[pl.ds(place * per_section, per_section)]
        else:
            owner = section ^ 1 if kind == "pair" else section
            target = layer_weight.at[pl.ds(owner * per_section, per_section)]
            if flip is not None:
                size = inputs[index].shape[1]
                target = target.at[:, pl.ds(pl.multiple_of((core ^ flip) * size, size), size)]
        return pltpu.make_async_copy(inputs[index], target, sems.at[index])

    for index in range(len(inputs)):
        copy(index).start()
    for slot in range(parts):
        line = pieces[slot][tile_area + rows :].astype(jnp.float32)
        notes[slot : slot + 1] = line[0:1].astype(jnp.int32)
    to_scalars = pltpu.make_async_copy(notes, plan, plan_sem)
    to_scalars.start()
    empty = jnp.zeros((rows, even.shape[1]), jnp.bfloat16)
    for state in states:
        state[0:rows] = empty
        state[(parts + 1) * rows : (parts + 2) * rows] = empty

    def slot_of(position):
        return position if in_order else position ^ own

    for slot in range(parts):
        position = slot_of(slots[slot])
        value = jnp.dot(pieces[slot][tile_area : tile_area + rows], entry_ref[...], preferred_element_type=jnp.float32)
        value = jnp.maximum(value, 0.0).astype(jnp.bfloat16)
        initial[position] = value
        even[pl.ds(pl.multiple_of((position + 1) * rows, rows), rows)] = value
    to_scalars.wait()

    def note(slot, index):
        if in_order:
            return plan[slot, index]
        found = plan[0, index]
        for which in range(1, parts):
            found = jnp.where(slot == slots[which], plan[which, index], found)
        return found

    for index, slot in enumerate(slots):
        position = slot_of(slot)
        before = slot_of(jnp.maximum(position - 1, 0))
        after = slot_of(jnp.minimum(position + 1, parts - 1))
        previous = [note(before, i) for i in range(listed_count)]
        following = [note(after, i) for i in range(listed_count)]
        band[position] = jnp.zeros(band.shape[1:], jnp.bfloat16)
        for block in range(blocks):
            for k in range(tile_count):
                source = plan[index, listed_count + block * tile_count + k]
                far = source - blocks
                column = blocks + source
                for i in range(listed_count):
                    column = jnp.where(far == i, previous[i], column)
                    column = jnp.where(far == listed_count + i, 2 * blocks + following[i], column)
                column = jnp.clip(column, 0, 3 * blocks - 1)
                start = pl.multiple_of(column * tile_rows, tile_rows)
                first = (block * tile_count + k) * tile_rows
                place = (position, slice(block * tile_rows, (block + 1) * tile_rows), pl.ds(start, tile_rows))
                band[place] += pieces[index][first : first + tile_rows]

    raised = [index for index, share in enumerate(shares) if share[0] == "up"]
    homes = [index for index, share in enumerate(shares) if share[0] != "up"]

    @pl.when(section >= lower)
    def _():
        for index in raised:
            copy(index).wait()

    @pl.when(section < lower)
    def _():
        for index in homes:
            copy(index).wait()

    depth = jnp.where(section < lower, lower * per_section, layers)
    for layer in range(layers):
        beta = math.log(decay_theta / (layer + 1) + 1.0)
        reach = depth - 1 - layer
        lowest = jnp.maximum(own - reach, 0)
        highest = jnp.minimum(own + reach + 1, parts)
        count = jnp.where(reach >= 0, highest - lowest, 0)
        before_ref, after_ref = states[layer % 2], states[(layer + 1) % 2]
        if layer == lower * per_section:

            @pl.when(section >= lower)
            def _():
                for index in homes:
                    copy(index).wait()

            @pl.when(section < lower)
            def _():
                for index in raised:
                    copy(index).wait()

        def support_of(position, before_ref=before_ref):
            window = before_ref[pl.ds(pl.multiple_of(position * rows, rows), 3 * rows)]
            aggregate = jnp.dot(band[position], window, preferred_element_type=jnp.float32)
            return (
                (1.0 - residual_share) * aggregate + residual_share * initial[position].astype(jnp.float32)
            ).astype(jnp.bfloat16)

        def finish(position, support, after_ref=after_ref, beta=beta, layer=layer):
            product = jnp.dot(support, layer_weight[layer], preferred_element_type=jnp.float32)
            mixed = (1.0 - beta) * support.astype(jnp.float32) + beta * product
            target = pl.ds(pl.multiple_of((position + 1) * rows, rows), rows)
            after_ref[target] = jnp.maximum(mixed, 0.0).astype(jnp.bfloat16)

        partial = count > 0
        if not in_order and 2 * (layers - 1 - layer) + 1 >= parts:
            partial = partial & (count < parts)

            @pl.when(count == parts)
            def _(support_of=support_of, finish=finish):
                for position in range(parts):
                    finish(position, support_of(position))

        @pl.when(partial)
        def _(support_of=support_of, finish=finish, lowest=lowest, highest=highest, count=count):
            first_support[...] = support_of(lowest)

            @pl.loop(0, count // 2)
            def _(pair):
                position = lowest + 2 * pair
                second_support[...] = support_of(position + 1)
                finish(position, first_support[...])
                first_support[...] = support_of(jnp.minimum(position + 2, highest - 1))
                finish(position + 1, second_support[...])

            @pl.when(count % 2 == 1)
            def _():
                finish(highest - 1, first_support[...])

        if (layer + 1) % per_section == 0:
            leaving = layer // per_section
            mine = pl.ds(pl.multiple_of((own + 1) * rows, rows), rows)

            @pl.when(section == leaving)
            def _():
                placed_ref[0, group] = after_ref[mine]

            @pl.when(section ^ 1 == leaving)
            def _():
                sent_ref[...] = after_ref[mine]


def shards(features, input_weight, layer_weights, tiles, pub_ids, tile_src):
    groups, rows, _ = features.shape
    _, blocks, tile_count, tile_rows, _ = tiles.shape
    listed_count = pub_ids.shape[1]
    per_section, width, _ = layer_weights.shape
    section, sections = lax.axis_index("section"), lax.axis_size("section")
    me, doms = lax.axis_index("dom"), lax.axis_size("dom")
    layers = per_section * sections
    core, group = me % 2, section % groups

    own_tiles = lax.dynamic_index_in_dim(tiles, group, 0, keepdims=False).reshape(-1, tile_rows)
    own_features = lax.dynamic_index_in_dim(features, group, 0, keepdims=False)
    own_ids = lax.dynamic_index_in_dim(pub_ids, group, 0, keepdims=False)
    own_sources = lax.dynamic_index_in_dim(tile_src, group, 0, keepdims=False).reshape(-1)
    notes = jnp.concatenate([own_ids, own_sources])
    notes = jnp.pad(notes.astype(jnp.bfloat16)[None], ((0, meta_rows - 1), (0, tile_rows - notes.shape[0])))
    payload = jnp.concatenate([own_tiles, own_features, notes], 0)
    payload, layer_weights = lax.optimization_barrier((payload, layer_weights))

    in_order = doms > layers or doms & (doms - 1) != 0
    lower = sections // 2
    senders = [(t, d) for t in range(lower) for d in range(doms)]
    route = [(t * doms + d, (lower + (t ^ d % 2)) * doms + d) for t, d in senders]
    half = width // 2
    my_share = lax.dynamic_slice_in_dim(layer_weights, core * half, half, 1)
    masks = () if in_order else range(2, doms, 2)
    far = [swapped(payload, "dom", mask) for mask in masks]
    up = one_way(layer_weights, ("section", "dom"), route)
    pair = swapped(my_share, "section", 1)
    mate = swapped(payload, "dom", 1)
    far, mate = lax.optimization_barrier((far, mate))
    if in_order:
        parts, own = 2 * layers + 1, jnp.int32(layers)
        slots = tuple(range(parts))
        pieces = [payload if d == 0 else shifted(payload, "dom", d) for d in range(-layers, layers + 1)]
    else:
        parts, own = doms, me
        slots, pieces = [0, 1], [payload, mate]
        for mask, piece in zip(masks, far):
            slots += [mask, mask + 1]
            pieces += [piece, swapped(piece, "dom", 1)]
        pair, _ = lax.optimization_barrier((pair, pieces[3::2]))
        slots = tuple(slots)
    inputs = [layer_weights, up, swapped(up, "dom", 1), pair, swapped(pair, "dom", 1)]
    shares = [("own", None), ("up", 0), ("up", 1), ("pair", 0), ("pair", 1)]
    place = jnp.stack([own, section, core, group]).astype(jnp.int32)

    dims = (
        parts, in_order, layers, per_section, blocks, tile_count, listed_count, tile_rows, rows, slots, tuple(shares), lower,
    )
    smem = pl.BlockSpec(memory_space=pltpu.SMEM)
    vmem = pl.BlockSpec(memory_space=pltpu.VMEM)
    anywhere = pl.BlockSpec(memory_space=pl.ANY)
    placed, sent = pl.pallas_call(
        functools.partial(cone_kernel, dims),
        out_shape=(
            jax.ShapeDtypeStruct((1, groups, rows, width), jnp.bfloat16),
            jax.ShapeDtypeStruct((rows, width), jnp.bfloat16),
        ),
        in_specs=[smem, vmem] + [vmem] * parts + [anywhere] * len(inputs),
        out_specs=(vmem, vmem),
        scratch_shapes=[
            pltpu.VMEM((layers, width, width), jnp.bfloat16),
            pltpu.VMEM((parts, rows, 3 * rows), jnp.bfloat16),
            pltpu.VMEM((parts, rows, width), jnp.bfloat16),
            pltpu.VMEM(((parts + 2) * rows, width), jnp.bfloat16),
            pltpu.VMEM(((parts + 2) * rows, width), jnp.bfloat16),
            pltpu.VMEM((rows, width), jnp.bfloat16),
            pltpu.VMEM((rows, width), jnp.bfloat16),
            pltpu.VMEM((parts, tile_rows), jnp.int32),
            pltpu.SMEM((parts, tile_rows), jnp.int32),
            pltpu.SemaphoreType.DMA((len(inputs),)),
            pltpu.SemaphoreType.DMA,
        ],
        compiler_params=pltpu.CompilerParams(vmem_limit_bytes=vmem_bytes),
    )(place, input_weight, *pieces, *inputs)
    other = swapped(sent, "section", 1)
    return lax.dynamic_update_slice(placed, other[None, None], (0, 1 - group, 0, 0))


def solution(mesh):
    in_specs = (
        P(None, "dom", None),
        P(),
        P("section", None, None),
        P(None, "dom", None, None, None),
        P(None, "dom"),
        P(None, "dom", None),
    )
    out_specs = P("section", None, "dom", None)
    return jax.shard_map(shards, mesh=mesh, in_specs=in_specs, out_specs=out_specs, check_vma=False)
```
